32 devices in a mesh: rep: 4 (over x, core), shard: 8 (over z, y).
Axes of the slice: x: 2, y: 2, z: 4, core: 2. Of those that a mesh axis runs over, the one named last changes fastest.
Arguments:
- inputs: bfloat16 [4, 2048, 1088], P('rep', 'shard'), may hold values from -6 to 6
- w_attn: bfloat16 [2, 1088, 3264], P(None, 'shard'), may hold values from -0.1875 to 0.1875
- w_out: bfloat16 [2, 1088, 1088], P(None, 'shard'), may hold values from -2 to 2
- w_fc: bfloat16 [2, 1088, 4352], P(None, 'shard'), may hold values from -0.1875 to 0.1875
- w_proj: bfloat16 [2, 4352, 1088], P(None, 'shard'), may hold values from -0.09375 to 0.09375
- norm_gains: float32 [2, 2, 1088], P(None, None, 'shard'), may hold values from 0.25 to 1.75
- norm_biases: float32 [2, 2, 1088], P(None, None, 'shard'), may hold values from -1.5 to 1.5
- dense_biases: float32 [2, 4, 1088], P(None, None, 'shard'), may hold values from -1.5 to 1.5
- fc_bias: float32 [2, 4352], P(None, 'shard'), may hold values from -2.5 to 2.5
- cotangent: bfloat16 [4, 2048, 1088], P('rep', 'shard'), may hold values from -6 to 6
Outputs:
- result: bfloat16 [4, 2048, 1088], P('rep', 'shard')
- input_grad: float32 [4, 2048, 1088], P('rep', 'shard')
- grad_w_attn: float32 [2, 1088, 3264], P(None, 'shard')
- grad_w_out: float32 [2, 1088, 1088], P(None, 'shard')
- grad_w_fc: float32 [2, 1088, 4352], P(None, 'shard')
- grad_w_proj: float32 [2, 4352, 1088], P(None, 'shard')
- grad_norm_gains: float32 [2, 2, 1088], P(None, None, 'shard')
- grad_norm_biases: float32 [2, 2, 1088], P(None, None, 'shard')
- grad_dense_biases: float32 [2, 4, 1088], P(None, None, 'shard')
- grad_fc_bias: float32 [2, 4352], P(None, 'shard')
The draws below stay inside these ranges and needn't reach their ends.
All inputs are finite; a program needn't handle non-finite values.
Results may differ from the reference program's by a relative error of at most 0.023.
Values may be sent and summed in bfloat16 or wider, within the bound.
A program may use at most 384 MiB of HBM per device.

```python
from functools import partial
import jax
import jax.numpy as jnp
from jax import lax

D = 1088
HEADS = 17
HEAD_SIZE = 64
FF = 4352
LAYERS = 2
SEQ_LEN = 2048
SEQS_ALL = 4


def block_scale(own_key, dims, split, low, largest):
    level, own = 1.0, jax.random.fold_in(own_key, 6)
    for position, shards_of in split:
        heights = jnp.exp(jax.random.uniform(jax.random.fold_in(own, position), (shards_of,), jnp.float32, low / len(split), largest / len(split)))
        level = level * jnp.repeat(heights, dims[position] // shards_of).reshape([-1 if axis == position else 1 for axis in range(len(dims))])
    return level


def gaussian(rng, dims, scale, reach, split=(), dtype=jnp.bfloat16):
    values = jax.random.normal(rng, dims, jnp.float32) * scale
    if len(split) > 0:
        values = block_scale(rng, dims, split, -0.22, 0.18) * values
    return jnp.clip(values, min=-reach, max=reach).astype(dtype)


def setup_inputs(seed: int = 0) -> dict:
    arg_keys = jax.random.split(jax.random.key(seed), 11)
    inputs = gaussian(arg_keys[0], (SEQS_ALL, SEQ_LEN, D), 1.0, 6.0, ((0, 4), (1, 8)))
    w_attn = gaussian(arg_keys[1], (LAYERS, D, 3 * D), D ** -0.5, 0.1875, ((1, 8),))
    w_out = gaussian(arg_keys[2], (LAYERS, D, D), (max(D // 128, 1)) ** -0.5, 2.0, ((1, 8),))
    w_fc = gaussian(arg_keys[3], (LAYERS, D, FF), D ** -0.5, 0.1875, ((1, 8),))
    w_proj = gaussian(arg_keys[4], (LAYERS, FF, D), FF ** -0.5, 0.09375, ((1, 8),))
    norm_gains = jnp.clip(1.0 + 0.15 * jax.random.normal(arg_keys[5], (LAYERS, 2, D), jnp.float32), 0.25, 1.75)
    norm_biases = gaussian(arg_keys[6], (LAYERS, 2, D), 0.3, 1.5, ((2, 8),), jnp.float32)
    dense_biases = gaussian(arg_keys[7], (LAYERS, 4, D), 0.3, 1.5, ((2, 8),), jnp.float32)
    fc_bias = gaussian(arg_keys[8], (LAYERS, FF), 0.5, 2.5, ((1, 8),), jnp.float32)
    cotangent = gaussian(arg_keys[9], (SEQS_ALL, SEQ_LEN, D), 1.0, 6.0, ((0, 4), (1, 8)))
    return dict(inputs=inputs, w_attn=w_attn, w_out=w_out, w_fc=w_fc, w_proj=w_proj, norm_gains=norm_gains, norm_biases=norm_biases, dense_biases=dense_biases, fc_bias=fc_bias, cotangent=cotangent)


eps = 1e-05
masked = -1e+30

@jax.custom_vjp
def low(v):
    return lax.optimization_barrier(v.astype(jnp.bfloat16)).astype(jnp.float32)

@jax.custom_vjp
def low_back(v):
    return v

def low_keep(v):
    return (low(v), None)

def low_pass(kept, grad):
    return (grad,)

def back_keep(v):
    return (v, None)

def back_low(kept, grad):
    return (low(grad),)
low.defvjp(low_keep, low_pass)
low_back.defvjp(back_keep, back_low)

def matmul(left, right):
    return jnp.dot(left, right, precision=lax.Precision.HIGHEST, preferred_element_type=jnp.float32)

def norm(x, gain, bias):
    centre = lax.optimization_barrier(jnp.mean(x, axis=-1, keepdims=True))
    centred = x - centre
    rstd = lax.rsqrt(lax.optimization_barrier(jnp.mean(centred * centred, axis=-1, keepdims=True)) + eps)
    return centred * rstd * gain + bias

def attention(query, keys, values):
    length = query.shape[0]
    block = min(512, length)
    scale = HEAD_SIZE ** (-0.5)
    key_pos = jnp.arange(length).astype(jnp.int32)

    def one_block(start):
        rows = lax.dynamic_slice_in_dim(query, start, block, 0)
        raw = low_back(jnp.einsum('qhe,khe->hqk', rows, keys, precision=lax.Precision.HIGHEST))
        scores = raw * scale
        query_pos = start + jnp.arange(block).astype(jnp.int32)
        allowed = key_pos[None, :] <= query_pos[:, None]
        scores = jnp.where(allowed[None], scores, masked)
        top = lax.optimization_barrier(jnp.max(scores, axis=-1, keepdims=True))
        expo = jnp.exp(scores - top)
        weights = expo / lax.optimization_barrier(jnp.sum(expo, axis=-1, keepdims=True))
        return jnp.einsum('hqk,khe->qhe', low(weights), values, precision=lax.Precision.HIGHEST)
    starts = (jnp.arange(length // block) * block).astype(jnp.int32)
    joined = lax.map(jax.checkpoint(one_block), starts)
    return joined.reshape(length, HEADS * HEAD_SIZE)

def split_heads(tensor):
    return tensor.reshape(tensor.shape[0], HEADS, HEAD_SIZE)

def block(x, w_attn, w_out, w_fc, w_proj, gains, shifts, dense, fc_shift):
    width = x.shape[1]
    normed = low(norm(x, gains[0], shifts[0]))
    mixed = low_back(matmul(normed, w_attn))
    query = low(mixed[:, :width] + dense[0])
    keys = low(mixed[:, width:2 * width])
    values = low(mixed[:, 2 * width:] + dense[1])
    attended = low(low_back(attention(split_heads(query), split_heads(keys), split_heads(values))))
    middle = x + low_back(matmul(attended, w_out)) + dense[2]
    normed2 = low(norm(middle, gains[1], shifts[1]))
    hidden = low_back(matmul(normed2, w_fc)) + fc_shift
    active = low(jax.nn.gelu(hidden, approximate=True))
    return middle + low_back(matmul(active, w_proj)) + dense[3]

def forward(inputs, w_attn, w_out, w_fc, w_proj, norm_gains, norm_biases, dense_biases, fc_bias):
    state = inputs
    for layer in range(LAYERS):
        step = partial(block, w_attn=w_attn[layer], w_out=w_out[layer], w_fc=w_fc[layer], w_proj=w_proj[layer], gains=norm_gains[layer], shifts=norm_biases[layer], dense=dense_biases[layer], fc_shift=fc_bias[layer])
        state = lax.map(step, state)
    return state

def reference(inputs, w_attn, w_out, w_fc, w_proj, norm_gains, norm_biases, dense_biases, fc_bias, cotangent):
    result, pullback = jax.vjp(forward, inputs.astype(jnp.float32), w_attn.astype(jnp.float32), w_out.astype(jnp.float32), w_fc.astype(jnp.float32), w_proj.astype(jnp.float32), norm_gains, norm_biases, dense_biases, fc_bias)
    grads = pullback(cotangent.astype(jnp.float32))
    return (result.astype(jnp.bfloat16), grads[0], grads[1], grads[2], grads[3], grads[4], grads[5], grads[6], grads[7], grads[8])
```

```python
import jax
import jax.numpy as jnp
from jax import lax
from jax.sharding import PartitionSpec as P

HEADS = 17
HEAD_SIZE = 64
LAYERS = 2
SCALE = HEAD_SIZE ** (-0.5)

eps = 1e-05
masked = -1e30
low = jnp.bfloat16


def norm_forward(x, gain, bias):
    centre = jnp.mean(x, axis=-1, keepdims=True)
    centred = x - centre
    rstd = lax.rsqrt(jnp.mean(centred * centred, axis=-1, keepdims=True) + eps)
    normal = centred * rstd
    return (normal * gain + bias, (normal, rstd))


def norm_backward(grad, saved, gain):
    normal, rstd = saved
    scaled = grad * gain
    gain_grad = jnp.sum(grad * normal, axis=0)
    bias_grad = jnp.sum(grad, axis=0)
    inner = scaled - jnp.mean(scaled, axis=-1, keepdims=True)
    inner = inner - normal * jnp.mean(scaled * normal, axis=-1, keepdims=True)
    return (rstd * inner, gain_grad, bias_grad)


def dot(left, right, left_dim, right_dim):
    return lax.dot_general(
        left, right, (((left_dim,), (right_dim,)), ((), ())), preferred_element_type=jnp.float32
    )


def gather_tokens(block, seqs, span):
    whole = lax.all_gather(block.reshape(seqs, span, -1), "shard", axis=1, tiled=True)
    return whole.reshape(-1, block.shape[-1])


def scatter_tokens(partial, seqs):
    part = lax.psum_scatter(
        partial.astype(low).reshape(seqs, -1, partial.shape[-1]),
        "shard",
        scatter_dimension=1,
        tiled=True,
    )
    return part.reshape(-1, partial.shape[-1]).astype(jnp.float32)


def swap(blocks):
    return lax.all_to_all(blocks, "shard", split_axis=0, concat_axis=0, tiled=True)


def query_blocks(length):
    size = 512 if length % 512 == 0 else length
    return [(start, size) for start in range(0, length, size)]


def block_scores(query, keys, start, size):
    end = start + size
    scores = jnp.einsum("bqd,bkd->bqk", query, keys, preferred_element_type=jnp.float32) * SCALE
    query_pos = start + jnp.arange(size, dtype=jnp.int32)
    key_pos = jnp.arange(end, dtype=jnp.int32)
    return scores, (key_pos[None, :] <= query_pos[:, None])[None]


def attend_forward(query, keys, values):
    mixed, logsum = [], []
    for start, size in query_blocks(query.shape[1]):
        end = start + size
        scores, allowed = block_scores(query[:, start:end], keys[:, :end], start, size)
        scores = jnp.where(allowed, scores, masked)
        top = jnp.max(scores, axis=-1, keepdims=True)
        probs = jnp.exp(scores - top)
        total = jnp.sum(probs, axis=-1, keepdims=True)
        out = jnp.einsum(
            "bqk,bkd->bqd", probs.astype(low), values[:, :end], preferred_element_type=jnp.float32
        )
        mixed.append(out / total)
        logsum.append(top + jnp.log(total))
    return jnp.concatenate(mixed, axis=1), logsum


def attend_backward(query, keys, values, grad_out, logsum, delta):
    length = query.shape[1]
    query_grad = []
    key_grad = jnp.zeros(keys.shape, jnp.float32)
    value_grad = jnp.zeros(values.shape, jnp.float32)
    for block, (start, size) in enumerate(query_blocks(length)):
        end = start + size
        rows, cols = query[:, start:end], keys[:, :end]
        grad_rows = grad_out[:, start:end]
        scores, allowed = block_scores(rows, cols, start, size)
        probs = jnp.where(allowed, jnp.exp(scores - logsum[block]), 0.0)
        prob_grad = jnp.einsum(
            "bqd,bkd->bqk", grad_rows, values[:, :end], preferred_element_type=jnp.float32
        )
        score_grad = (probs * (prob_grad - delta[:, start:end]) * SCALE).astype(low)
        query_grad.append(
            jnp.einsum("bqk,bkd->bqd", score_grad, cols, preferred_element_type=jnp.float32)
        )
        key_add = jnp.einsum("bqk,bqd->bkd", score_grad, rows, preferred_element_type=jnp.float32)
        value_add = jnp.einsum(
            "bqk,bqd->bkd", probs.astype(low), grad_rows, preferred_element_type=jnp.float32
        )
        pad = ((0, 0), (0, length - end), (0, 0))
        key_grad = key_grad + jnp.pad(key_add, pad)
        value_grad = value_grad + jnp.pad(value_add, pad)
    return jnp.concatenate(query_grad, axis=1), key_grad, value_grad


def body(
    inputs, w_attn, w_out, w_fc, w_proj, norm_gains, norm_biases, dense_biases, fc_bias, cotangent
):
    seqs, span, width = inputs.shape
    count = lax.axis_size("shard")
    reps = lax.axis_size("rep")
    index = lax.axis_index("shard")
    length = span * count
    rows = w_attn.shape[1]
    own_heads = -(-HEADS // count)
    group = own_heads * HEAD_SIZE
    padded = group * count
    hidden_own = fc_bias.shape[1]

    def pad_last(array):
        return jnp.pad(array, [(0, 0)] * (array.ndim - 1) + [(0, padded - width)])

    def to_heads(flat):
        tensor = flat.reshape(seqs, length, own_heads, HEAD_SIZE).transpose(0, 2, 1, 3)
        return tensor.reshape(seqs * own_heads, length, HEAD_SIZE)

    def from_heads(tensor):
        flat = tensor.reshape(seqs, own_heads, length, HEAD_SIZE).transpose(0, 2, 1, 3)
        return flat.reshape(seqs * length, group)

    columns = []
    for layer in range(LAYERS):
        pieces = [
            pad_last(w_attn[layer][:, part * width : (part + 1) * width]).reshape(
                rows, count, group
            )
            for part in range(3)
        ]
        pieces.append(w_fc[layer].reshape(rows, count, hidden_own))
        send = jnp.concatenate(pieces, axis=2).transpose(1, 0, 2)
        columns.append(swap(send).reshape(rows * count, -1))

    vectors = jnp.concatenate([norm_gains, norm_biases, dense_biases], axis=1)
    vectors = lax.all_gather(vectors.reshape(LAYERS * 8, -1), "shard", axis=0, tiled=False)
    vectors = vectors.transpose(1, 0, 2).reshape(LAYERS, 8, width)
    vectors = lax.optimization_barrier(vectors)

    def own_part(vector):
        return lax.dynamic_slice_in_dim(pad_last(vector), index * group, group, 0)

    def spread(part):
        whole = lax.dynamic_update_slice_in_dim(
            jnp.zeros((padded,), part.dtype), part, index * group, 0
        )
        return whole[:width]

    state = inputs.reshape(seqs * span, width).astype(jnp.float32)
    stored = []
    for layer in range(LAYERS):
        vec = vectors[layer]
        attn_cols = columns[layer][:, : 3 * group]
        fc_cols = columns[layer][:, 3 * group :]
        out_full = lax.all_gather(w_out[layer], "shard", axis=0, tiled=True)
        normed, saved_one = norm_forward(state, vec[0], vec[2])
        normed_all = gather_tokens(normed.astype(low), seqs, span)
        mixed = dot(normed_all, attn_cols, 1, 0)
        query = to_heads((mixed[:, :group] + own_part(vec[4])).astype(low))
        keys = to_heads(mixed[:, group : 2 * group].astype(low))
        values = to_heads((mixed[:, 2 * group :] + own_part(vec[5])).astype(low))
        attended, logsum = attend_forward(query, keys, values)
        send = from_heads(attended.astype(low)).reshape(seqs, count, span, group)
        joined = swap(send.transpose(1, 0, 2, 3)).transpose(1, 2, 0, 3)
        attended_low = joined.reshape(seqs * span, padded)[:, :width]
        middle = state + dot(attended_low, out_full, 1, 0) + vec[6]
        normed2, saved_two = norm_forward(middle, vec[1], vec[3])
        normed2_all = gather_tokens(normed2.astype(low), seqs, span)
        hidden = dot(normed2_all, fc_cols, 1, 0) + fc_bias[layer]
        active_low = jax.nn.gelu(hidden, approximate=True).astype(low)
        state = middle + scatter_tokens(dot(active_low, w_proj[layer], 1, 0), seqs) + vec[7]
        stored.append(
            (
                attn_cols, fc_cols, out_full, saved_one, normed_all, query, keys, values,
                attended, logsum, attended_low, saved_two, normed2_all, hidden, active_low,
            )
        )
    result = state.reshape(seqs, span, width).astype(low)

    grad = cotangent.reshape(seqs * span, width).astype(jnp.float32)
    grads = [None] * LAYERS
    small = [None] * LAYERS
    fc_small = [None] * LAYERS
    for layer in reversed(range(LAYERS)):
        (
            attn_cols, fc_cols, out_full, saved_one, normed_all, query, keys, values,
            attended, logsum, attended_low, saved_two, normed2_all, hidden, active_low,
        ) = stored[layer]
        vec = vectors[layer]
        proj_bias_grad = jnp.sum(grad, axis=0)
        grad_all = gather_tokens(grad.astype(low), seqs, span)
        active_grad = dot(grad_all, w_proj[layer], 1, 1)
        gelu_pull = jax.vjp(lambda value: jax.nn.gelu(value, approximate=True), hidden)[1]
        hidden_grad = gelu_pull(active_grad)[0]
        fc_small[layer] = jnp.sum(hidden_grad, axis=0)
        hidden_low = hidden_grad.astype(low)
        normed2_grad = scatter_tokens(dot(hidden_low, fc_cols, 1, 1), seqs)
        proj_grad = dot(active_low, grad_all, 0, 0).astype(low)
        fc_grad = dot(normed2_all, hidden_low, 0, 0).astype(low)
        middle_norm, gain_two, shift_two = norm_backward(normed2_grad, saved_two, vec[1])
        middle_grad = grad + middle_norm
        out_bias_grad = jnp.sum(middle_grad, axis=0)
        middle_low = middle_grad.astype(low)
        attended_grad = pad_last(dot(middle_low, out_full, 1, 1).astype(low))
        send = attended_grad.reshape(seqs, span, count, group).transpose(2, 0, 1, 3)
        grad_heads = to_heads(swap(send).transpose(1, 0, 2, 3).reshape(seqs * length, group))
        out_grad = lax.psum_scatter(
            dot(attended_low, middle_low, 0, 0).astype(low),
            "shard",
            scatter_dimension=0,
            tiled=True,
        )
        delta = jnp.sum(grad_heads.astype(jnp.float32) * attended, axis=-1, keepdims=True)
        query_grad, key_grad, value_grad = attend_backward(
            query, keys, values, grad_heads, logsum, delta
        )
        query_bias = spread(jnp.sum(query_grad.reshape(seqs, own_heads, length, HEAD_SIZE), axis=(0, 2)).reshape(group))
        value_bias = spread(jnp.sum(value_grad.reshape(seqs, own_heads, length, HEAD_SIZE), axis=(0, 2)).reshape(group))
        mixed_low = jnp.concatenate(
            [from_heads(part.astype(low)) for part in (query_grad, key_grad, value_grad)], axis=1
        )
        normed_grad = scatter_tokens(dot(mixed_low, attn_cols, 1, 1), seqs)
        attn_grad = dot(normed_all, mixed_low, 0, 0).astype(low)
        input_norm, gain_one, shift_one = norm_backward(normed_grad, saved_one, vec[0])
        grad = middle_grad + input_norm

        small[layer] = jnp.stack(
            [gain_one, gain_two, shift_one, shift_two, query_bias, value_bias, out_bias_grad, proj_bias_grad]
        )
        by_cols = jnp.concatenate([attn_grad, fc_grad], axis=1)
        part_cols = by_cols.shape[1] // reps
        by_cols = by_cols.reshape(count * rows, reps, part_cols).transpose(1, 0, 2)
        by_cols = lax.psum_scatter(by_cols, "rep", scatter_dimension=0, tiled=False)
        by_cols = swap(by_cols.reshape(count, rows, part_cols))
        by_cols = lax.all_gather(by_cols, "rep", axis=0, tiled=False)
        by_cols = by_cols.transpose(2, 1, 0, 3).reshape(rows, count, reps * part_cols)
        attn_rows = [
            by_cols[:, :, part * group : (part + 1) * group].reshape(rows, padded)[:, :width]
            for part in range(3)
        ]
        attn_grad = jnp.concatenate(attn_rows, axis=1).astype(jnp.float32)
        fc_grad = by_cols[:, :, 3 * group :].reshape(rows, -1).astype(jnp.float32)
        by_rows = jnp.concatenate([proj_grad, out_grad], axis=0)
        by_rows = by_rows.reshape(-1, reps, width // reps).transpose(1, 0, 2)
        by_rows = lax.psum_scatter(by_rows, "rep", scatter_dimension=0, tiled=False)
        by_rows = lax.all_gather(by_rows, "rep", axis=0, tiled=False)
        by_rows = by_rows.transpose(1, 0, 2).reshape(-1, width).astype(jnp.float32)
        grads[layer] = (attn_grad, by_rows[hidden_own:], fc_grad, by_rows[:hidden_own])

    stacked = [jnp.stack([grads[layer][item] for layer in range(LAYERS)]) for item in range(4)]
    little = lax.psum(jnp.stack(small), ("rep", "shard"))
    little = lax.dynamic_slice_in_dim(little, index * rows, rows, 2)
    fc_little = lax.psum(jnp.stack(fc_small), "rep")
    return (
        result,
        grad.reshape(seqs, span, width),
        stacked[0],
        stacked[1],
        stacked[2],
        stacked[3],
        little[:, 0:2],
        little[:, 2:4],
        little[:, 4:8],
        fc_little,
    )


def solution(mesh):
    tokens = P("rep", "shard", None)
    weight = P(None, "shard", None)
    vector = P(None, None, "shard")
    in_specs = (
        tokens, weight, weight, weight, weight, vector, vector, vector, P(None, "shard"), tokens,
    )
    out_specs = (
        tokens, tokens, weight, weight, weight, weight, vector, vector, vector, P(None, "shard"),
    )
    return jax.shard_map(body, mesh=mesh, in_specs=in_specs, out_specs=out_specs, check_vma=False)
```

```python
import jax
import jax.numpy as jnp
from jax import lax
from jax.sharding import PartitionSpec as P

HEADS = 17
HEAD_SIZE = 64
LAYERS = 2
SCALE = HEAD_SIZE ** (-0.5)

eps = 1e-05
masked = -1e30
low = jnp.bfloat16


def norm_forward(x, gain, bias):
    centre = jnp.mean(x, axis=-1, keepdims=True)
    centred = x - centre
    rstd = lax.rsqrt(jnp.mean(centred * centred, axis=-1, keepdims=True) + eps)
    normal = centred * rstd
    return (normal * gain + bias, (normal, rstd))


def norm_backward(grad, saved, gain):
    normal, rstd = saved
    scaled = grad * gain
    gain_grad = jnp.sum(grad * normal, axis=0)
    bias_grad = jnp.sum(grad, axis=0)
    inner = scaled - jnp.mean(scaled, axis=-1, keepdims=True)
    inner = inner - normal * jnp.mean(scaled * normal, axis=-1, keepdims=True)
    return (rstd * inner, gain_grad, bias_grad)


def dot(left, right, left_dim, right_dim):
    return lax.dot_general(
        left, right, (((left_dim,), (right_dim,)), ((), ())), preferred_element_type=jnp.float32
    )


def gather_tokens(block, seqs, span):
    whole = lax.all_gather(block.reshape(seqs, span, -1), "shard", axis=1, tiled=True)
    return whole.reshape(-1, block.shape[-1])


def gather_reps(block):
    return lax.all_gather(block, "rep", axis=0, tiled=True)


def scatter_reps(partial):
    part = lax.psum_scatter(partial.astype(low), "rep", scatter_dimension=0, tiled=True)
    return part.astype(jnp.float32)


def scatter_rows(partial):
    return lax.psum_scatter(partial.astype(low), "shard", scatter_dimension=0, tiled=True)


def scatter_tokens(partial, seqs):
    part = lax.psum_scatter(
        partial.astype(low).reshape(seqs, -1, partial.shape[-1]),
        "shard",
        scatter_dimension=1,
        tiled=True,
    )
    return part.reshape(-1, partial.shape[-1]).astype(jnp.float32)


def swap(blocks):
    return lax.all_to_all(blocks, "shard", split_axis=0, concat_axis=0, tiled=True)


def query_blocks(length):
    size = 512 if length % 512 == 0 else length
    return [(start, size) for start in range(0, length, size)]


def block_scores(query, keys, start, size):
    end = start + size
    scores = jnp.einsum("bqd,bkd->bqk", query, keys, preferred_element_type=jnp.float32) * SCALE
    query_pos = start + jnp.arange(size, dtype=jnp.int32)
    key_pos = jnp.arange(end, dtype=jnp.int32)
    return scores, (key_pos[None, :] <= query_pos[:, None])[None]


def attend_forward(query, keys, values):
    mixed, logsum = [], []
    for start, size in query_blocks(query.shape[1]):
        end = start + size
        scores, allowed = block_scores(query[:, start:end], keys[:, :end], start, size)
        scores = jnp.where(allowed, scores, masked)
        top = jnp.max(scores, axis=-1, keepdims=True)
        probs = jnp.exp(scores - top)
        total = jnp.sum(probs, axis=-1, keepdims=True)
        out = jnp.einsum(
            "bqk,bkd->bqd", probs.astype(low), values[:, :end], preferred_element_type=jnp.float32
        )
        mixed.append(out / total)
        logsum.append(top + jnp.log(total))
    return jnp.concatenate(mixed, axis=1), logsum


def attend_backward(query, keys, values, grad_out, logsum, delta):
    length = query.shape[1]
    query_grad = []
    key_grad = jnp.zeros(keys.shape, jnp.float32)
    value_grad = jnp.zeros(values.shape, jnp.float32)
    for block, (start, size) in enumerate(query_blocks(length)):
        end = start + size
        rows, cols = query[:, start:end], keys[:, :end]
        grad_rows = grad_out[:, start:end]
        scores, allowed = block_scores(rows, cols, start, size)
        probs = jnp.where(allowed, jnp.exp(scores - logsum[block]), 0.0)
        prob_grad = jnp.einsum(
            "bqd,bkd->bqk", grad_rows, values[:, :end], preferred_element_type=jnp.float32
        )
        score_grad = (probs * (prob_grad - delta[:, start:end]) * SCALE).astype(low)
        query_grad.append(
            jnp.einsum("bqk,bkd->bqd", score_grad, cols, preferred_element_type=jnp.float32)
        )
        key_add = jnp.einsum("bqk,bqd->bkd", score_grad, rows, preferred_element_type=jnp.float32)
        value_add = jnp.einsum(
            "bqk,bqd->bkd", probs.astype(low), grad_rows, preferred_element_type=jnp.float32
        )
        pad = ((0, 0), (0, length - end), (0, 0))
        key_grad = key_grad + jnp.pad(key_add, pad)
        value_grad = value_grad + jnp.pad(value_add, pad)
    return jnp.concatenate(query_grad, axis=1), key_grad, value_grad


def body(
    inputs, w_attn, w_out, w_fc, w_proj, norm_gains, norm_biases, dense_biases, fc_bias, cotangent
):
    seqs, span, width = inputs.shape
    count = lax.axis_size("shard")
    reps = lax.axis_size("rep")
    index = lax.axis_index("shard")
    length = span * count
    rows = w_attn.shape[1]
    own_heads = -(-HEADS // count)
    group = own_heads * HEAD_SIZE
    padded = group * count
    replica = lax.axis_index("rep")
    hidden_own = fc_bias.shape[1] // reps
    quarter = 3 * group // reps

    def pad_last(array):
        return jnp.pad(array, [(0, 0)] * (array.ndim - 1) + [(0, padded - width)])

    def to_heads(flat):
        tensor = flat.reshape(seqs, length, own_heads, HEAD_SIZE).transpose(0, 2, 1, 3)
        return tensor.reshape(seqs * own_heads, length, HEAD_SIZE)

    def from_heads(tensor):
        flat = tensor.reshape(seqs, own_heads, length, HEAD_SIZE).transpose(0, 2, 1, 3)
        return flat.reshape(seqs * length, group)

    def of_replica(array, axis, size):
        return lax.dynamic_slice_in_dim(array, replica * size, size, axis)

    vectors = jnp.concatenate(
        [norm_gains, norm_biases, dense_biases, of_replica(fc_bias, 1, hidden_own)[:, None]], axis=1
    )
    vectors = lax.all_gather(vectors.reshape(LAYERS * 9, -1), "shard", axis=0, tiled=False)
    vectors = vectors.transpose(1, 0, 2).reshape(LAYERS, 9, width)
    vectors = lax.optimization_barrier(vectors)

    columns = []
    for layer in range(LAYERS):
        pieces = [
            pad_last(w_attn[layer][:, part * width : (part + 1) * width]).reshape(
                rows, count, group
            )
            for part in range(3)
        ]
        send = jnp.concatenate(pieces, axis=2).transpose(1, 0, 2)
        mine = lax.all_gather(swap(of_replica(send, 2, quarter)), "rep", axis=0, tiled=False)
        attn_cols = mine.transpose(1, 2, 0, 3).reshape(rows * count, 3 * group)
        fc_part = of_replica(w_fc[layer].reshape(rows, count, -1), 2, hidden_own)
        fc_cols = lax.all_gather(
            fc_part.reshape(rows, count * hidden_own), "shard", axis=0, tiled=True
        )
        proj_rows = lax.all_gather(
            of_replica(w_proj[layer], 0, hidden_own), "shard", axis=0, tiled=True
        )
        out_full = lax.all_gather(w_out[layer], "shard", axis=0, tiled=True)
        columns.append((attn_cols, out_full, fc_cols, proj_rows))

    def own_part(vector):
        return lax.dynamic_slice_in_dim(pad_last(vector), index * group, group, 0)

    def spread(part):
        whole = lax.dynamic_update_slice_in_dim(
            jnp.zeros((padded,), part.dtype), part, index * group, 0
        )
        return whole[:width]

    state = inputs.reshape(seqs * span, width).astype(jnp.float32)
    stored = []
    for layer in range(LAYERS):
        vec = vectors[layer]
        attn_cols, out_full, fc_cols, proj_rows = columns[layer]
        normed, saved_one = norm_forward(state, vec[0], vec[2])
        normed_all = gather_tokens(normed.astype(low), seqs, span)
        mixed = dot(normed_all, attn_cols, 1, 0)
        query = to_heads((mixed[:, :group] + own_part(vec[4])).astype(low))
        keys = to_heads(mixed[:, group : 2 * group].astype(low))
        values = to_heads((mixed[:, 2 * group :] + own_part(vec[5])).astype(low))
        attended, logsum = attend_forward(query, keys, values)
        send = from_heads(attended.astype(low)).reshape(seqs, count, span, group)
        joined = swap(send.transpose(1, 0, 2, 3)).transpose(1, 2, 0, 3)
        attended_low = joined.reshape(seqs * span, padded)[:, :width]
        middle = state + dot(attended_low, out_full, 1, 0) + vec[6]
        normed2, saved_two = norm_forward(middle, vec[1], vec[3])
        normed2_all = gather_reps(normed2.astype(low))
        hidden = dot(normed2_all, fc_cols, 1, 0) + vec[8]
        active_low = jax.nn.gelu(hidden, approximate=True).astype(low)
        state = middle + scatter_reps(dot(active_low, proj_rows, 1, 0)) + vec[7]
        stored.append(
            (
                saved_one, normed_all, query, keys, values,
                attended, logsum, attended_low, saved_two, normed2_all, hidden, active_low,
            )
        )
    result = state.reshape(seqs, span, width).astype(low)

    grad = cotangent.reshape(seqs * span, width).astype(jnp.float32)
    grads = [None] * LAYERS
    small = [None] * LAYERS
    for layer in reversed(range(LAYERS)):
        (
            saved_one, normed_all, query, keys, values,
            attended, logsum, attended_low, saved_two, normed2_all, hidden, active_low,
        ) = stored[layer]
        attn_cols, out_full, fc_cols, proj_rows = columns[layer]
        vec = vectors[layer]
        proj_bias_grad = jnp.sum(grad, axis=0)
        grad_all = gather_reps(grad.astype(low))
        active_grad = dot(grad_all, proj_rows, 1, 1)
        gelu_pull = jax.vjp(lambda value: jax.nn.gelu(value, approximate=True), hidden)[1]
        hidden_grad = gelu_pull(active_grad)[0]
        fc_bias_grad = jnp.sum(hidden_grad, axis=0)
        hidden_low = hidden_grad.astype(low)
        normed2_grad = scatter_reps(dot(hidden_low, fc_cols, 1, 1))
        proj_grad = scatter_rows(dot(active_low, grad_all, 0, 0))
        fc_grad = scatter_rows(dot(normed2_all, hidden_low, 0, 0))
        middle_norm, gain_two, shift_two = norm_backward(normed2_grad, saved_two, vec[1])
        middle_grad = grad + middle_norm
        out_bias_grad = jnp.sum(middle_grad, axis=0)
        middle_low = middle_grad.astype(low)
        attended_grad = pad_last(dot(middle_low, out_full, 1, 1).astype(low))
        send = attended_grad.reshape(seqs, span, count, group).transpose(2, 0, 1, 3)
        grad_heads = to_heads(swap(send).transpose(1, 0, 2, 3).reshape(seqs * length, group))
        out_grad = dot(attended_low, middle_low, 0, 0).astype(low)
        delta = jnp.sum(grad_heads.astype(jnp.float32) * attended, axis=-1, keepdims=True)
        query_grad, key_grad, value_grad = attend_backward(
            query, keys, values, grad_heads, logsum, delta
        )
        query_bias = spread(jnp.sum(query_grad.reshape(seqs, own_heads, length, HEAD_SIZE), axis=(0, 2)).reshape(group))
        value_bias = spread(jnp.sum(value_grad.reshape(seqs, own_heads, length, HEAD_SIZE), axis=(0, 2)).reshape(group))
        mixed_low = jnp.concatenate(
            [from_heads(part.astype(low)) for part in (query_grad, key_grad, value_grad)], axis=1
        )
        normed_grad = scatter_tokens(dot(mixed_low, attn_cols, 1, 1), seqs)
        attn_grad = dot(normed_all, mixed_low, 0, 0).astype(low)
        input_norm, gain_one, shift_one = norm_backward(normed_grad, saved_one, vec[0])
        grad = middle_grad + input_norm

        small[layer] = jnp.stack(
            [gain_one, gain_two, shift_one, shift_two, query_bias, value_bias, out_bias_grad, proj_bias_grad, fc_bias_grad]
        )
        both = jnp.concatenate(
            [
                attn_grad.reshape(width, reps, quarter),
                out_grad.reshape(width, reps, width // reps),
            ],
            axis=2,
        ).transpose(1, 0, 2)
        both = lax.psum_scatter(both, "rep", scatter_dimension=0, tiled=False)
        attn_part = swap(both[:, :quarter].reshape(count, rows, quarter))
        attn_part = attn_part.transpose(1, 0, 2).reshape(rows, count * quarter)
        out_part = lax.psum_scatter(
            both[:, quarter:], "shard", scatter_dimension=0, tiled=True
        )
        early = lax.all_gather(jnp.stack([proj_grad.reshape(-1), fc_grad.reshape(-1)]), "rep", axis=0)
        proj_grad = early[:, 0].reshape(reps * hidden_own, width).astype(jnp.float32)
        fc_grad = early[:, 1].reshape(reps, rows, count, hidden_own).transpose(1, 2, 0, 3)
        fc_grad = fc_grad.reshape(rows, -1).astype(jnp.float32)
        late = lax.all_gather(jnp.concatenate([attn_part, out_part], axis=1), "rep", axis=0)
        out_grad = late[:, :, count * quarter :].transpose(1, 0, 2).reshape(rows, width)
        by_heads = late[:, :, : count * quarter].reshape(reps, rows, count, quarter)
        by_heads = by_heads.transpose(1, 2, 0, 3).reshape(rows, count, 3 * group)
        attn_rows = [
            by_heads[:, :, part * group : (part + 1) * group].reshape(rows, padded)[:, :width]
            for part in range(3)
        ]
        attn_grad = jnp.concatenate(attn_rows, axis=1).astype(jnp.float32)
        grads[layer] = (attn_grad, out_grad.astype(jnp.float32), fc_grad, proj_grad)

    stacked = [jnp.stack([grads[layer][item] for layer in range(LAYERS)]) for item in range(4)]
    little = jnp.stack(small).reshape(LAYERS * 9, count, rows).transpose(1, 0, 2)
    little = jnp.sum(swap(little), axis=0).reshape(LAYERS, 9, rows)
    fc_little = lax.dynamic_update_slice_in_dim(
        jnp.zeros((LAYERS, reps, rows), jnp.float32), little[:, 8:], replica, 1
    )
    little = lax.psum(jnp.concatenate([little[:, :8], fc_little], axis=1), "rep")
    fc_little = little[:, 8:].reshape(LAYERS, reps * rows)
    return (
        result,
        grad.reshape(seqs, span, width),
        stacked[0],
        stacked[1],
        stacked[2],
        stacked[3],
        little[:, 0:2],
        little[:, 2:4],
        little[:, 4:8],
        fc_little,
    )


def solution(mesh):
    tokens = P("rep", "shard", None)
    weight = P(None, "shard", None)
    vector = P(None, None, "shard")
    in_specs = (
        tokens, weight, weight, weight, weight, vector, vector, vector, P(None, "shard"), tokens,
    )
    out_specs = (
        tokens, tokens, weight, weight, weight, weight, vector, vector, vector, P(None, "shard"),
    )
    return jax.shard_map(body, mesh=mesh, in_specs=in_specs, out_specs=out_specs, check_vma=False)
```
